32 devices in a mesh: space: 16 (over z, x, core), spec: 2 (over y).
Axes of the slice: x: 2, y: 2, z: 4, core: 2. Of those that a mesh axis runs over, the one named last changes fastest.
Arguments:
- tracers: float32 [240, 8, 128, 384], P('spec', None, 'space'), may hold values from 0.1 to 10
- courant: float32 [2, 8, 128, 384], P(None, None, 'space'), may hold values from -0.9 to 0.9
- layer_mass: float32 [8, 128, 384], P(None, 'space'), may hold values from 0.5 to 2
- pbl_top: int32 [128, 384], P('space'), may hold values from 1 to 8
- land_type: int32 [128, 384], P('space'), may hold values from 0 to 10
- rates: float32 [11, 240], replicated, may hold values from 0.05 to 3
- coupling: float32 [240, 240], replicated, may hold values from -0.375 to 0.375
Outputs:
- updated: float32 [240, 8, 128, 384], P('spec', None, 'space')
- deposited: float32 [240, 128, 384], P('spec', 'space')
The draws below stay inside these ranges and needn't reach their ends.
All inputs are finite; a program needn't handle non-finite values.
Results may differ from the reference program's by a relative error of at most 0.0003.
Values sent between devices are 32-bit elements; how exact they have to be, the bound alone decides.
A program may use at most 192 MiB of HBM per device.

```python
import math
import jax
import jax.numpy as jnp
from jax import lax

SPECIES = 240
LEVELS = 8
LAND = 11
STEPS = 2
NY = 384
NX = 128
N_SPEC = 2


def place_ends(entries, key, low, top_value):
    dims = entries.shape
    spot = [jax.random.randint(jax.random.fold_in(key, axis), (), 0, dims[axis]) for axis in range(len(dims))]
    entries = entries.at[tuple(spot)].set(low)
    longest = dims.index(max(dims))
    spot[longest] = (spot[longest] + 1) % dims[longest]
    return entries.at[tuple(spot)].set(top_value)


def level_of(own_key, shape, shards, low, high):
    factor_of, own = 1.0, jax.random.fold_in(own_key, 6)
    for dim, shards_of in shards:
        draws = jnp.exp(jax.random.uniform(jax.random.fold_in(own, dim), (shards_of,), jnp.float32, low / len(shards), high / len(shards)))
        factor_of = factor_of * jnp.repeat(draws, shape[dim] // shards_of).reshape([-1 if axis == dim else 1 for axis in range(len(shape))])
    return factor_of


def centred(rng, extent, spread, bound, held_as=jnp.bfloat16):
    result = jax.random.normal(rng, extent, jnp.float32) * spread
    return jnp.minimum(jnp.maximum(result, -bound), bound).astype(held_as)


def setup_inputs(seed: int = 0) -> dict:
    splits = jax.random.split(jax.random.key(seed), 8)
    return {
        "tracers": jnp.clip(jnp.exp(math.log(10.0) - 4.6051702 * jax.random.uniform(splits[0], (SPECIES, LEVELS, NX, NY), jnp.float32) ** level_of(splits[0], (SPECIES, LEVELS, NX, NY), ((0, 2), (2, 16)), -0.2, 0.2)), 0.1, 10.0),
        "courant": jnp.clip(jax.random.uniform(splits[1], (2, LEVELS, NX, NY), jnp.float32, -0.9, 0.9) * level_of(splits[1], (2, LEVELS, NX, NY), ((2, 16),), -0.4, 0.0), -0.9, 0.9),
        "layer_mass": jnp.clip(jnp.exp(math.log(2.0) - 1.3862944 * jax.random.uniform(splits[2], (LEVELS, NX, NY), jnp.float32) ** level_of(splits[2], (LEVELS, NX, NY), ((1, 16),), -0.2, 0.2)), 0.5, 2.0),
        "pbl_top": place_ends(jax.random.randint(splits[3], (NX, NY), 1, LEVELS + 1), jax.random.fold_in(splits[3], 1), 1, LEVELS).astype(jnp.int32),
        "land_type": place_ends(jax.random.randint(splits[4], (NX, NY), 0, LAND), jax.random.fold_in(splits[4], 1), 0, LAND - 1).astype(jnp.int32),
        "rates": jnp.clip(jnp.exp(jax.random.uniform(splits[5], (LAND, SPECIES), jnp.float32, math.log(0.05), math.log(3.0))), 0.05, 3.0),
        "coupling": centred(splits[6], (SPECIES, SPECIES), SPECIES ** -0.5, 0.375, jnp.float32),
    }


def sweep(field, speed, axis):
    count = field.shape[axis]

    def cut(a, lo, hi):
        return lax.slice_in_dim(a, lo, hi, axis=axis)

    edge = (7.0 / 12.0) * (cut(field, 1, count - 2) + cut(field, 2, count - 1)) - (1.0 / 12.0) * (cut(field, 0, count - 3) + cut(field, 3, count))
    lower = cut(edge, 0, count - 4)
    upper = cut(edge, 1, count - 3)
    centre = cut(field, 2, count - 2)
    slope = upper - lower
    curve = 6.0 * (centre - 0.5 * (lower + upper))
    cells = count - 4
    face = cut(speed, 3, count - 2)
    upwind = face * (cut(upper, 0, cells - 1) - 0.5 * face * (cut(slope, 0, cells - 1) - (1.0 - 2.0 * face / 3.0) * cut(curve, 0, cells - 1)))
    downwind = face * (cut(lower, 1, cells) - 0.5 * face * (cut(slope, 1, cells) + (1.0 + 2.0 * face / 3.0) * cut(curve, 1, cells)))
    flux = jnp.where(face >= 0.0, upwind, downwind)
    return cut(field, 3, count - 3) - (cut(flux, 1, count - 5) - cut(flux, 0, count - 6))


def advect(block, courant):
    for step in range(STEPS):
        padded = jnp.pad(block, ((0, 0), (0, 0), (3, 3), (0, 0)))
        speed = jnp.pad(courant[0], ((0, 0), (3, 3), (0, 0)))
        block = sweep(padded, speed, -2)
        padded = jnp.pad(block, ((0, 0), (0, 0), (0, 0), (3, 3)))
        speed = jnp.pad(courant[1], ((0, 0), (0, 0), (3, 3)))
        block = sweep(padded, speed, -1)
    return block


def mixing(field, layer_mass, pbl_top):
    levels = jnp.arange(field.shape[1], dtype=jnp.int32)[:, None, None]
    inside = levels < pbl_top[None]
    weights = jnp.where(inside, layer_mass, 0.0)
    average = jnp.sum(weights[None] * field, axis=1) / jnp.sum(weights, axis=0)[None]
    return jnp.where(inside[None], average[:, None], field)


def deposit(field, surface_mass, land_type, rates):
    kinds = jnp.arange(rates.shape[0], dtype=jnp.int32)[:, None]
    onehot = (land_type.reshape(1, -1) == kinds).astype(jnp.float32)
    loss = jnp.dot(rates.T, onehot, precision=lax.Precision.HIGHEST).reshape(field.shape[0], field.shape[2], field.shape[3])
    bottom = field[:, 0]
    kept = bottom * jnp.exp(-loss)
    return field.at[:, 0].set(kept), (bottom - kept) * surface_mass[None]


def reference(tracers, courant, layer_mass, pbl_top, land_type, rates, coupling):
    groups = tracers.reshape(N_SPEC, SPECIES // N_SPEC, LEVELS, NX, NY)
    advected = lax.map(lambda block: advect(block, courant), groups).reshape(SPECIES, LEVELS, NX, NY)
    mixed = mixing(advected, layer_mass, pbl_top)
    coupled = mixed + jnp.dot(coupling, mixed.reshape(SPECIES, -1), precision=lax.Precision.HIGHEST).reshape(mixed.shape)
    updated, deposited = deposit(coupled, layer_mass[0], land_type, rates)
    return updated, deposited
```

```python
import functools

import jax
import jax.numpy as jnp
from jax import lax
from jax.experimental import pallas as pl
from jax.experimental.pallas import tpu as pltpu
from jax.sharding import PartitionSpec as P

HALO = 6


def flux_weights(c):
    a = 0.5 * c
    ab = a * (1.0 - 2.0 * c / 3.0)
    high, low, own = 1.0 - a - 3.0 * ab, a - 3.0 * ab, 6.0 * ab
    up = [
        -low / 12.0,
        (7.0 * low - high) / 12.0,
        7.0 * (low + high) / 12.0 + own,
        (7.0 * high - low) / 12.0,
        -high / 12.0,
        jnp.zeros_like(c),
    ]
    ab = a * (1.0 + 2.0 * c / 3.0)
    low, high, own = 1.0 + a + 3.0 * ab, 3.0 * ab - a, -6.0 * ab
    down = [
        jnp.zeros_like(c),
        -low / 12.0,
        (7.0 * low - high) / 12.0,
        7.0 * (low + high) / 12.0 + own,
        (7.0 * high - low) / 12.0,
        -high / 12.0,
    ]
    return [c * jnp.where(c >= 0.0, u, d) for u, d in zip(up, down)]


def sweep_weights(below, above):
    lo, hi = flux_weights(below), flux_weights(above)
    weights = []
    for k in range(-3, 4):
        w = jnp.ones_like(below) if k == 0 else jnp.zeros_like(below)
        if -2 <= k <= 3:
            w = w - hi[k + 2]
        if -3 <= k <= 2:
            w = w + lo[k + 3]
        weights.append(w)
    return weights


def transport_kernel(group, tracers, before, after, wx, wy, wm, out, ext, mid):
    rows = wm.shape[0]
    lanes = wm.shape[2]

    def rows_of(ref, r):
        acc = wx[0, r[0]] * ref[r[1]]
        for k in range(1, 7):
            acc = acc + wx[k, r[0]] * ref[r[1] + k]
        return acc

    def lanes_of(q, r):
        left = pltpu.roll(q, 1, 1)
        right = pltpu.roll(q, lanes - 1, 1)
        total = wy[3, r] * q + wy[2, r] * left + wy[4, r] * right
        total = total + pltpu.roll(wy[0, r] * q + wy[1, r] * right, 3, 1)
        return total + pltpu.roll(wy[6, r] * q + wy[5, r] * left, lanes - 3, 1)

    def one(s, _):
        ext[0:HALO] = before[s]
        ext[HALO : HALO + rows] = jnp.transpose(tracers[s], (1, 0, 2))
        ext[HALO + rows :] = after[s]
        for r in range(rows + 6):
            mid[r] = lanes_of(rows_of(ext, (r, r)), r)
        for r in range(rows):
            q = lanes_of(rows_of(mid, (r + 3, r)), r + 3)
            share = wm[r]
            mean = jnp.sum(share * q, axis=0, keepdims=True)
            ext[r] = jnp.where(share > 0.0, mean, q)
        out[s] = jnp.transpose(ext[0:rows], (1, 0, 2))
        return 0

    lax.fori_loop(0, group, one, 0)


def transport(chunk, start, tracers, before, after, wx, wy, wm):
    levels, rows, lanes = tracers.shape[1:]
    group = max(g for g in (1, 2, 3, 5, 6) if chunk % g == 0)
    first = start // group

    def whole(array):
        return pl.BlockSpec(array.shape, lambda i: (0,) * array.ndim)

    return pl.pallas_call(
        functools.partial(transport_kernel, group),
        grid=(chunk // group,),
        out_shape=jax.ShapeDtypeStruct((chunk, levels, rows, lanes), jnp.float32),
        in_specs=[
            pl.BlockSpec((group, levels, rows, lanes), lambda i: (i + first, 0, 0, 0)),
            pl.BlockSpec((group, HALO, levels, lanes), lambda i: (i, 0, 0, 0)),
            pl.BlockSpec((group, HALO, levels, lanes), lambda i: (i, 0, 0, 0)),
            whole(wx),
            whole(wy),
            whole(wm),
        ],
        out_specs=pl.BlockSpec((group, levels, rows, lanes), lambda i: (i, 0, 0, 0)),
        scratch_shapes=[
            pltpu.VMEM((rows + 2 * HALO, levels, lanes), jnp.float32),
            pltpu.VMEM((rows + 6, levels, lanes), jnp.float32),
        ],
        compiler_params=pltpu.CompilerParams(vmem_limit_bytes=24 * 1024 * 1024),
        cost_estimate=pl.CostEstimate(
            flops=chunk * levels * (4 * rows + 12) * lanes * 15,
            bytes_accessed=chunk * levels * (2 * rows + 2 * HALO) * lanes * 4,
            transcendentals=0,
        ),
    )(tracers, before, after, wx, wy, wm)


def neighbours(last, leading, axis):
    devices = lax.axis_size(axis)
    up = [(i, i + 1) for i in range(devices - 1)]
    down = [(i + 1, i) for i in range(devices - 1)]
    return lax.ppermute(last, axis, up), lax.ppermute(leading, axis, down)


def on_device(tracers, courant, layer_mass, pbl_top, land_type, rates, coupling):
    species, levels, rows, lanes = tracers.shape
    parts, place = lax.axis_size("spec"), lax.axis_index("spec")
    strips, strip = lax.axis_size("space"), lax.axis_index("space")

    before, after = neighbours(courant[:, :, rows - 3 :], courant[:, :, :4], "space")
    pieces = max(n for n in (1, 2, 3, 4, 5) if species % n == 0)
    chunk = species // pieces
    halos = []
    for piece in range(pieces):
        block = tracers[piece * chunk : (piece + 1) * chunk]
        last, leading = block[:, :, rows - HALO :], block[:, :, :HALO]
        if piece:
            tie = (before, after) if piece == 1 else halos[piece - 2]
            *tie, last, leading = lax.optimization_barrier((*tie, last, leading))
            if piece == 1:
                before, after = tie
            else:
                halos[piece - 2] = tuple(tie)
        halos.append(
            neighbours(
                jnp.transpose(last, (0, 2, 1, 3)),
                jnp.transpose(leading, (0, 2, 1, 3)),
                "space",
            )
        )
    speed = jnp.transpose(jnp.concatenate([before, courant, after], axis=2), (0, 2, 1, 3))
    row = strip * rows + jnp.arange(-3, rows + 3)
    exists = ((row >= 0) & (row < strips * rows))[:, None, None]
    wx = jnp.stack(
        [jnp.where(exists, w, 0.0) for w in sweep_weights(speed[0, :-1], speed[0, 1:])]
    )
    along = speed[1, :-1]
    above = jnp.pad(along[:, :, 1:], ((0, 0), (0, 0), (0, 1)))
    lane = jnp.arange(lanes)
    wy = []
    for k, w in zip(range(-3, 4), sweep_weights(along, above)):
        w = jnp.where((lane + k >= 0) & (lane + k < lanes), w, 0.0)
        wy.append(jnp.roll(w, -3 if k < -1 else 3 if k > 1 else 0, axis=-1))
    wy = jnp.stack(wy)
    inside = jnp.arange(levels, dtype=jnp.int32)[:, None, None] < pbl_top[None]
    share = jnp.where(inside, layer_mass, 0.0)
    wm = jnp.transpose(share / jnp.sum(share, axis=0, keepdims=True), (1, 0, 2))

    mine, theirs = [], [[] for _ in range(parts - 1)]
    for piece in range(pieces):
        mixed = transport(chunk, piece * chunk, tracers, *halos[piece], wx, wy, wm)
        mine.append(mixed)
        for away in range(1, parts):
            theirs[away - 1].append(
                lax.ppermute(mixed, "spec", [(i, (i + away) % parts) for i in range(parts)])
            )

    matrix = lax.dynamic_slice_in_dim(coupling, place * species, species, 0)

    def times_all(away, fields):
        source = lax.rem(place + parts - away, parts)
        part = lax.dynamic_slice_in_dim(matrix, source * species, species, 1)
        field = jnp.concatenate(fields, axis=0)
        return jnp.einsum("ij,jlrx->ilrx", part, field, precision=lax.Precision.HIGH)

    coupled = jnp.concatenate(mine, axis=0) + times_all(0, mine)
    for away in range(1, parts):
        coupled = coupled + times_all(away, theirs[away - 1])

    own_rates = lax.dynamic_slice_in_dim(rates, place * species, species, 1)
    kinds = jnp.arange(rates.shape[0], dtype=jnp.int32)[:, None]
    onehot = (land_type.reshape(1, -1) == kinds).astype(jnp.float32)
    loss = jnp.dot(own_rates.T, onehot, precision=lax.Precision.HIGHEST)
    keep = jnp.exp(-loss.reshape(species, rows, lanes))
    bottom = coupled[:, 0]
    kept = bottom * keep
    level = jnp.arange(levels)[None, :, None, None]
    updated = jnp.where(level == 0, kept[:, None], coupled)
    return updated, (bottom - kept) * layer_mass[0][None]


def solution(mesh):
    return jax.shard_map(
        on_device,
        mesh=mesh,
        in_specs=(
            P("spec", None, "space", None),
            P(None, None, "space", None),
            P(None, "space", None),
            P("space", None),
            P("space", None),
            P(),
            P(),
        ),
        out_specs=(P("spec", None, "space", None), P("spec", "space", None)),
        check_vma=False,
    )
```

```python
import functools

import jax
import jax.numpy as jnp
from jax import lax
from jax.experimental import pallas as pl
from jax.experimental.pallas import tpu as pltpu
from jax.sharding import PartitionSpec as P

HALO = 6


def flux_weights(c):
    a = 0.5 * c
    ab = a * (1.0 - 2.0 * c / 3.0)
    high, low, own = 1.0 - a - 3.0 * ab, a - 3.0 * ab, 6.0 * ab
    up = [
        -low / 12.0,
        (7.0 * low - high) / 12.0,
        7.0 * (low + high) / 12.0 + own,
        (7.0 * high - low) / 12.0,
        -high / 12.0,
        jnp.zeros_like(c),
    ]
    ab = a * (1.0 + 2.0 * c / 3.0)
    low, high, own = 1.0 + a + 3.0 * ab, 3.0 * ab - a, -6.0 * ab
    down = [
        jnp.zeros_like(c),
        -low / 12.0,
        (7.0 * low - high) / 12.0,
        7.0 * (low + high) / 12.0 + own,
        (7.0 * high - low) / 12.0,
        -high / 12.0,
    ]
    return [c * jnp.where(c >= 0.0, u, d) for u, d in zip(up, down)]


def sweep_weights(below, above):
    lo, hi = flux_weights(below), flux_weights(above)
    weights = []
    for k in range(-3, 4):
        w = jnp.ones_like(below) if k == 0 else jnp.zeros_like(below)
        if -2 <= k <= 3:
            w = w - hi[k + 2]
        if -3 <= k <= 2:
            w = w + lo[k + 3]
        weights.append(w)
    return weights


def transport_kernel(group, tracers, before, after, wx, wy, wm, out, ext, mid):
    rows = wm.shape[0]
    lanes = wm.shape[2]

    def rows_of(ref, r):
        acc = wx[0, r[0]] * ref[r[1]]
        for k in range(1, 7):
            acc = acc + wx[k, r[0]] * ref[r[1] + k]
        return acc

    def lanes_of(q, r):
        left = pltpu.roll(q, 1, 1)
        right = pltpu.roll(q, lanes - 1, 1)
        total = wy[3, r] * q + wy[2, r] * left + wy[4, r] * right
        total = total + pltpu.roll(wy[0, r] * q + wy[1, r] * right, 3, 1)
        return total + pltpu.roll(wy[6, r] * q + wy[5, r] * left, lanes - 3, 1)

    def one(s, _):
        ext[0:HALO] = before[s]
        ext[HALO : HALO + rows] = jnp.transpose(tracers[s], (1, 0, 2))
        ext[HALO + rows :] = after[s]
        for r in range(rows + 6):
            mid[r] = lanes_of(rows_of(ext, (r, r)), r)
        for r in range(rows):
            q = lanes_of(rows_of(mid, (r + 3, r)), r + 3)
            share = wm[r]
            mean = jnp.sum(share * q, axis=0, keepdims=True)
            ext[r] = jnp.where(share > 0.0, mean, q)
        out[s] = jnp.transpose(ext[0:rows], (1, 0, 2))
        return 0

    lax.fori_loop(0, group, one, 0)


def transport(chunk, start, tracers, before, after, wx, wy, wm):
    levels, rows, lanes = tracers.shape[1:]
    group = max(g for g in (1, 2, 3, 5, 6) if chunk % g == 0)
    first = start // group

    def whole(array):
        return pl.BlockSpec(array.shape, lambda i: (0,) * array.ndim)

    return pl.pallas_call(
        functools.partial(transport_kernel, group),
        grid=(chunk // group,),
        out_shape=jax.ShapeDtypeStruct((chunk, levels, rows, lanes), jnp.float32),
        in_specs=[
            pl.BlockSpec((group, levels, rows, lanes), lambda i: (i + first, 0, 0, 0)),
            pl.BlockSpec((group, HALO, levels, lanes), lambda i: (i, 0, 0, 0)),
            pl.BlockSpec((group, HALO, levels, lanes), lambda i: (i, 0, 0, 0)),
            whole(wx),
            whole(wy),
            whole(wm),
        ],
        out_specs=pl.BlockSpec((group, levels, rows, lanes), lambda i: (i, 0, 0, 0)),
        scratch_shapes=[
            pltpu.VMEM((rows + 2 * HALO, levels, lanes), jnp.float32),
            pltpu.VMEM((rows + 6, levels, lanes), jnp.float32),
        ],
        compiler_params=pltpu.CompilerParams(vmem_limit_bytes=24 * 1024 * 1024),
        cost_estimate=pl.CostEstimate(
            flops=chunk * levels * (4 * rows + 12) * lanes * 15,
            bytes_accessed=chunk * levels * (2 * rows + 2 * HALO) * lanes * 4,
            transcendentals=0,
        ),
    )(tracers, before, after, wx, wy, wm)


def neighbours(last, leading, axis):
    devices = lax.axis_size(axis)
    up = [(i, i + 1) for i in range(devices - 1)]
    down = [(i + 1, i) for i in range(devices - 1)]
    return lax.ppermute(last, axis, up), lax.ppermute(leading, axis, down)


def on_device(tracers, courant, layer_mass, pbl_top, land_type, rates, coupling):
    species, levels, rows, lanes = tracers.shape
    parts, place = lax.axis_size("spec"), lax.axis_index("spec")
    strips, strip = lax.axis_size("space"), lax.axis_index("space")

    before, after = neighbours(courant[:, :, rows - 3 :], courant[:, :, :4], "space")
    pieces = max(n for n in (1, 2, 3, 4, 5) if species % n == 0)
    chunk = species // pieces

    def halo(field, piece):
        block = field[piece * chunk : (piece + 1) * chunk]
        return neighbours(
            jnp.transpose(block[:, :, rows - HALO :], (0, 2, 1, 3)),
            jnp.transpose(block[:, :, :HALO], (0, 2, 1, 3)),
            "space",
        )

    halos = [halo(tracers, 0)]
    if pieces > 1:
        before, after, field = lax.optimization_barrier((before, after, tracers))
        halos.append(halo(field, 1))
    speed = jnp.transpose(jnp.concatenate([before, courant, after], axis=2), (0, 2, 1, 3))
    row = strip * rows + jnp.arange(-3, rows + 3)
    exists = ((row >= 0) & (row < strips * rows))[:, None, None]
    wx = jnp.stack(
        [jnp.where(exists, w, 0.0) for w in sweep_weights(speed[0, :-1], speed[0, 1:])]
    )
    along = speed[1, :-1]
    above = jnp.pad(along[:, :, 1:], ((0, 0), (0, 0), (0, 1)))
    lane = jnp.arange(lanes)
    wy = []
    for k, w in zip(range(-3, 4), sweep_weights(along, above)):
        w = jnp.where((lane + k >= 0) & (lane + k < lanes), w, 0.0)
        wy.append(jnp.roll(w, -3 if k < -1 else 3 if k > 1 else 0, axis=-1))
    wy = jnp.stack(wy)
    inside = jnp.arange(levels, dtype=jnp.int32)[:, None, None] < pbl_top[None]
    share = jnp.where(inside, layer_mass, 0.0)
    wm = jnp.transpose(share / jnp.sum(share, axis=0, keepdims=True), (1, 0, 2))

    mine, theirs = [], [[] for _ in range(parts - 1)]
    for piece in range(pieces):
        mixed = transport(chunk, piece * chunk, tracers, *halos[piece], wx, wy, wm)
        mine.append(mixed)
        for away in range(1, parts):
            theirs[away - 1].append(
                lax.ppermute(mixed, "spec", [(i, (i + away) % parts) for i in range(parts)])
            )
        if piece + 2 < pieces:
            mine[piece], field = lax.optimization_barrier((mixed, field))
            halos.append(halo(field, piece + 2))

    matrix = lax.dynamic_slice_in_dim(coupling, place * species, species, 0)

    def times_all(away, fields):
        source = lax.rem(place + parts - away, parts)
        part = lax.dynamic_slice_in_dim(matrix, source * species, species, 1)
        field = jnp.concatenate(fields, axis=0)
        return jnp.einsum("ij,jlrx->ilrx", part, field, precision=lax.Precision.HIGH)

    coupled = jnp.concatenate(mine, axis=0) + times_all(0, mine)
    for away in range(1, parts):
        coupled = coupled + times_all(away, theirs[away - 1])

    own_rates = lax.dynamic_slice_in_dim(rates, place * species, species, 1)
    kinds = jnp.arange(rates.shape[0], dtype=jnp.int32)[:, None]
    onehot = (land_type.reshape(1, -1) == kinds).astype(jnp.float32)
    loss = jnp.dot(own_rates.T, onehot, precision=lax.Precision.HIGHEST)
    keep = jnp.exp(-loss.reshape(species, rows, lanes))
    bottom = coupled[:, 0]
    kept = bottom * keep
    level = jnp.arange(levels)[None, :, None, None]
    updated = jnp.where(level == 0, kept[:, None], coupled)
    return updated, (bottom - kept) * layer_mass[0][None]


def solution(mesh):
    return jax.shard_map(
        on_device,
        mesh=mesh,
        in_specs=(
            P("spec", None, "space", None),
            P(None, None, "space", None),
            P(None, "space", None),
            P("space", None),
            P("space", None),
            P(),
            P(),
        ),
        out_specs=(P("spec", None, "space", None), P("spec", "space", None)),
        check_vma=False,
    )
```
